128 devices in a mesh: store: 8 (over x, core), sku: 16 (over z, y).
Axes of the slice: x: 4, y: 4, z: 4, core: 2. Of those that a mesh axis runs over, the one named last changes fastest.
Arguments:
- base_bottom: float32 [128, 13, 16384], P(('store', 'sku')), may hold values from -6 to 6
- weight_bottom: float32 [128, 13, 16384], P(('store', 'sku')), may hold values from 0.5 to 4
- base_category: float32 [128, 13, 1024], P(('store', 'sku')), may hold values from -24 to 24
- weight_category: float32 [128, 13, 1024], P(('store', 'sku')), may hold values from 0.02 to 0.2
- base_region: float32 [32, 13, 16384], P(None, None, ('store', 'sku')), may hold values from -24 to 24
- weight_region: float32 [32, 13, 16384], P(None, None, ('store', 'sku')), may hold values from 0.02 to 0.2
- category_map: int32 [16384], replicated, may hold values from 0 to 1023
- region_map: int32 [128], replicated, may hold values from 0 to 31
Outputs:
- reconciled: float32 [128, 13, 16384], P(('store', 'sku'))
- residual: float32 [128, 13, 16384], P(('store', 'sku'))
The draws below stay inside these ranges and needn't reach their ends.
All inputs are finite; a program needn't handle non-finite values.
Results may differ from the reference program's by a relative error of at most 0.0003.
Values sent between devices are 32-bit elements; how exact they have to be, the bound alone decides.
A program may use at most 128 MiB of HBM per device.

```python
import math
import jax
import jax.numpy as jnp

H = 13
NCAT = 1024
REGIONS = 32
ITERS = 3
STORE = 128
SKU = 16384


def set_ends(entries, stream_key, low, top_value):
    place = [jax.random.randint(jax.random.fold_in(stream_key, axis), (), 0, length) for axis, length in enumerate(entries.shape)]
    widest = entries.shape.index(max(entries.shape))
    neighbour = place[:widest] + [(place[widest] + 1) % entries.shape[widest]] + place[widest + 1:]
    return entries.at[tuple(place)].set(low).at[tuple(neighbour)].set(top_value)


def block_scale(rng, dims, pieces, least, top_value):
    loudness, own = 1.0, jax.random.fold_in(rng, 6)
    for dim, shards_of in pieces:
        heights = jnp.exp(jax.random.uniform(jax.random.fold_in(own, dim), (shards_of,), jnp.float32, least / len(pieces), top_value / len(pieces)))
        loudness = loudness * jnp.repeat(heights, dims[dim] // shards_of).reshape([-1 if axis == dim else 1 for axis in range(len(dims))])
    return loudness


def normal_values(own_key, shape, scale, limit, shards=(), kind=jnp.bfloat16):
    loudness = block_scale(own_key, shape, shards, -0.22, 0.18) if shards else 1.0
    result = jax.random.normal(own_key, shape, jnp.float32) * scale * loudness
    return jnp.minimum(jnp.maximum(result, -limit), limit).astype(kind)


def setup_inputs(seed: int = 0) -> dict:
    keys = jax.random.split(jax.random.key(seed), 9)
    base_bottom = normal_values(keys[0], (STORE, H, SKU), 1.0, 6.0, ((0, 128),), jnp.float32)
    weight_bottom = jnp.clip(jnp.exp(math.log(4.0) - 2.0794415 * jax.random.uniform(keys[1], (STORE, H, SKU), jnp.float32) ** block_scale(keys[1], (STORE, H, SKU), ((0, 128),), -0.2, 0.2)), 0.5, 4.0)
    base_category = normal_values(keys[2], (STORE, H, NCAT), 4.0, 24.0, ((0, 128),), jnp.float32)
    weight_category = jnp.clip(jnp.exp(math.log(0.2) - 2.3025851 * jax.random.uniform(keys[3], (STORE, H, NCAT), jnp.float32) ** block_scale(keys[3], (STORE, H, NCAT), ((0, 128),), -0.2, 0.2)), 0.02, 0.2)
    base_region = normal_values(keys[4], (REGIONS, H, SKU), 4.0, 24.0, ((2, 128),), jnp.float32)
    weight_region = jnp.clip(jnp.exp(math.log(0.2) - 2.3025851 * jax.random.uniform(keys[5], (REGIONS, H, SKU), jnp.float32) ** block_scale(keys[5], (REGIONS, H, SKU), ((2, 128),), -0.2, 0.2)), 0.02, 0.2)
    category_map = set_ends(jax.random.randint(keys[6], (SKU,), 0, NCAT), jax.random.fold_in(keys[6], 1), 0, NCAT - 1).astype(jnp.int32)
    region_map = set_ends(jax.random.randint(keys[7], (STORE,), 0, REGIONS), jax.random.fold_in(keys[7], 1), 0, REGIONS - 1).astype(jnp.int32)
    return {"base_bottom": base_bottom, "weight_bottom": weight_bottom, "base_category": base_category, "weight_category": weight_category, "base_region": base_region, "weight_region": weight_region, "category_map": category_map, "region_map": region_map}


def category_sums(field, category_map):
    moved = jnp.transpose(field, (2, 0, 1))
    summed = jax.ops.segment_sum(moved, category_map, num_segments=NCAT)
    return jnp.transpose(summed, (1, 2, 0))


def category_spread(values, category_map):
    return jnp.take(values, category_map, axis=2)


def region_sums(field, region_map):
    return jax.ops.segment_sum(field, region_map, num_segments=REGIONS)


def region_spread(values, region_map):
    return jnp.take(values, region_map, axis=0)


def reference(base_bottom, weight_bottom, base_category, weight_category, base_region, weight_region, category_map, region_map):
    def operate(field):
        first = category_spread(weight_category * category_sums(field, category_map), category_map)
        second = region_spread(weight_region * region_sums(field, region_map), region_map)
        return weight_bottom * field + first + second

    reconciled = base_bottom
    residual = category_spread(weight_category * (base_category - category_sums(base_bottom, category_map)), category_map)
    residual = residual + region_spread(weight_region * (base_region - region_sums(base_bottom, region_map)), region_map)
    direction = residual
    norm_now = jnp.sum(residual * residual)
    for repeat in range(ITERS):
        image = operate(direction)
        step_size = norm_now / jnp.sum(direction * image)
        reconciled = reconciled + step_size * direction
        residual = residual - step_size * image
        norm_next = jnp.sum(residual * residual)
        direction = residual + (norm_next / norm_now) * direction
        norm_now = norm_next
    return reconciled, residual
```

```python
import functools

import jax
import jax.numpy as jnp
from jax import lax
from jax.experimental import pallas as pl
from jax.experimental.pallas import tpu as pltpu
from jax.sharding import PartitionSpec as P

MESH = pl.DeviceIdType.MESH
F32, BF16 = jnp.float32, jnp.bfloat16
INNER = 256
WIDTH = 512


def split3(x):
    hi = x.astype(BF16)
    rest = x - hi.astype(F32)
    mid = rest.astype(BF16)
    low = (rest - mid.astype(F32)).astype(BF16)
    return hi, mid, low


def two_sum(a, b):
    s = a + b
    t = s - a
    return s, (a - (s - t)) + (b - t)


def two_product(a, b):
    p = a * b
    ta, tb = a * 4097.0, b * 4097.0
    ah, bh = ta - (ta - a), tb - (tb - b)
    al, bl = a - ah, b - bh
    return p, ((ah * bh - p) + ah * bl + al * bh) + al * bl


def pair_add(a, b):
    s, e = two_sum(a[0], b[0])
    e = e + (a[1] + b[1])
    high = s + e
    return high, e - (high - s)


def pair_mul(a, b):
    p, e = two_product(a[0], b[0])
    e = e + (a[0] * b[1] + a[1] * b[0])
    high = p + e
    return high, e - (high - p)


def pair_neg(a):
    return -a[0], -a[1]


def pair_div(a, b):
    q1 = a[0] / b[0]
    zero = jnp.zeros_like(q1)
    r = pair_add(a, pair_neg(pair_mul((q1, zero), b)))
    q2 = r[0] / b[0]
    r = pair_add(r, pair_neg(pair_mul((q2, zero), b)))
    q3 = r[0] / b[0]
    high, low = two_sum(q1, q2)
    return pair_add((high, low), (q3, zero))


def step_coefficients(m):
    one = (jnp.ones_like(m[0][0]), jnp.zeros_like(m[0][0]))
    scale = pair_div(m[0], m[1])
    inv = pair_div(one, m[0])
    mu, power = [one, one], scale
    powers = [one, scale]
    for k in range(2, 6):
        power = pair_mul(power, scale)
        powers.append(power)
        mu.append(pair_mul(pair_mul(m[k], inv), power))
    rr1 = pair_add(mu[2], pair_neg(one))
    a1 = pair_div(rr1, pair_add(mu[3], pair_neg(pair_mul(mu[2], mu[2]))))
    g0, g1, g2 = one, pair_neg(pair_add(one, pair_mul(a1, mu[2]))), a1
    rr2 = pair_mul(g2, pair_add(pair_add(mu[2], pair_mul(g1, mu[3])), pair_mul(g2, mu[4])))
    b1 = pair_div(rr2, rr1)
    h0 = pair_add(g0, pair_mul(b1, mu[2]))
    h1 = pair_add(g1, pair_neg(b1))
    h2 = g2
    energy = pair_mul(
        h2, pair_add(pair_add(pair_mul(h0, mu[3]), pair_mul(h1, mu[4])), pair_mul(h2, mu[5]))
    )
    a2 = pair_div(rr2, energy)
    c1 = pair_mul(pair_add(g1, pair_neg(pair_mul(a2, h0))), powers[1])
    c2 = pair_mul(pair_add(g2, pair_neg(pair_mul(a2, h1))), powers[2])
    c3 = pair_mul(pair_neg(pair_mul(a2, h2)), powers[3])
    e0 = pair_mul(pair_add(pair_add(one, pair_mul(a1, mu[2])), pair_mul(a2, h0)), powers[1])
    e1 = pair_mul(pair_add(pair_mul(a2, h1), pair_neg(a1)), powers[2])
    e2 = pair_mul(pair_mul(a2, h2), powers[3])
    return [c[0] for c in (c1, c2, c3)], [e[0] for e in (e0, e1, e2)]


def kernel(
    ns, nk,
    bb, wb, bc, wc, br, wr, cm, rm,
    rec, res,
    oh, lx, la, acc, p0, v0, v1, u2, tt, q, recv, qs, breg, mom, erow, arow, ared,
    send_f, recv_f, send_q, recv_q, send_a, recv_a,
):
    n = ns * nk
    horizon, skus = bb.shape
    n_cat = bc.shape[1]
    regions, _, wide = br.shape
    blocks = n_cat // INNER
    rows = 16 * blocks
    group = nk * wide
    subs = group // WIDTH
    st, sk = lax.axis_index("store"), lax.axis_index("sku")
    me = st * nk + sk

    def flipped(x, count):
        bits = [k for k in range(10) if 2**k < count]
        return [sum((2**k * (1 - 2 * ((x // 2**k) % 2)) for k in bits if (t // 2**k) % 2), x) for t in range(count)]

    sk_of = flipped(sk, nk)

    def st_of(a):
        out = 0
        for k in range(10):
            if 2**k < ns:
                out = out + ((st // 2**k + a // 2**k) % 2) * 2**k
        return out

    barrier = pltpu.get_barrier_semaphore()

    def greet(a, c):
        ps = st_of(a)
        for b in range(nk):
            def one_signal():
                pl.semaphore_signal(barrier, inc=1, device_id=(ps, sk_of[b]), device_id_type=MESH)
            if b == 0:
                pl.when(a > 0)(one_signal)
            else:
                one_signal()
        return c

    lax.fori_loop(0, ns, greet, 0)

    def columns(index, width):
        return pl.ds(pl.multiple_of(index * width, width), width)

    def send_group(a, src_of, dst, send_sem, recv_sem):
        ps = st_of(a)
        for b in range(nk):
            src = src_of(ps * nk + sk_of[b])
            def remote():
                pltpu.make_async_remote_copy(
                    src_ref=src, dst_ref=dst, send_sem=send_sem, recv_sem=recv_sem,
                    device_id=(ps, sk_of[b]), device_id_type=MESH,
                ).start()
            if b == 0:
                pl.when(a > 0)(remote)
                @pl.when(a == 0)
                def _():
                    pltpu.make_async_copy(src, dst, recv_sem).start()
            else:
                remote()

    def send_out(f, field, a):
        send_group(a, lambda p: field.at[:, columns(p, wide)], recv.at[f, me], send_f.at[f], recv_f.at[f])

    def send_back(f):
        def step(a, c):
            send_group(
                a, lambda p: qs.at[f, p], q.at[f, :, columns(me, wide)], send_q.at[f], recv_q.at[f, st]
            )
            return c
        lax.fori_loop(0, ns, step, 0)

    def wait_out(f):
        pltpu.make_async_copy(recv.at[f], recv.at[f], recv_f.at[f]).wait()

    def wait_back(f, g):
        part = qs.at[f, pl.ds(0, nk)]
        pltpu.make_async_copy(part, part, recv_q.at[f, g]).wait()

    def fill(i, c):
        cols = columns(i, WIDTH)
        inner = cm[:, cols] % INNER
        ids = lax.broadcasted_iota(jnp.int32, (INNER, WIDTH), 0)
        oh[:, cols] = jnp.where(ids == inner, 1.0, 0.0).astype(BF16)
        return c

    lax.fori_loop(0, skus // WIDTH, fill, 0)
    lx[...] = jnp.zeros_like(lx)
    la[...] = jnp.zeros_like(la)
    mom[...] = jnp.zeros_like(mom)
    erow[...] = jnp.zeros_like(erow)
    region_hot = jnp.where(lax.broadcasted_iota(jnp.int32, (regions, n), 0) == rm[...], 1.0, 0.0)
    counts = jnp.sum(region_hot, axis=1, keepdims=True)
    gather3 = jnp.concatenate([region_hot.astype(BF16)] * 3, axis=1)
    eye = jnp.where(
        lax.broadcasted_iota(jnp.int32, (n, n), 0) == lax.broadcasted_iota(jnp.int32, (n, n), 1), 1.0, 0.0
    ).astype(BF16)
    spread3 = lax.dot_general(
        eye, jnp.concatenate([region_hot.astype(BF16)] * 3, axis=0), (((1,), (1,)), ((), ())),
        preferred_element_type=F32,
    ).astype(BF16)

    def category_add(x, cols):
        outer = cm[:, cols] // INNER
        for piece, part in enumerate(split3(x)):
            part = part.astype(F32)
            for m in range(blocks):
                lx[pl.ds(rows * piece + 16 * m, horizon), :] = jnp.where(outer == m, part, 0.0).astype(BF16)
        acc[...] += lax.dot_general(
            lx[...], oh[:, cols], (((1,), (1,)), ((), ())), preferred_element_type=F32
        )

    def category_total(m):
        return (
            acc[pl.ds(16 * m, horizon), :]
            + acc[pl.ds(rows + 16 * m, horizon), :]
            + acc[pl.ds(2 * rows + 16 * m, horizon), :]
        )

    def spread_set(m, values):
        for piece, part in enumerate(split3(values)):
            la[pl.ds(rows * piece + 16 * m, horizon), :] = part

    def category_spread(cols):
        outer = cm[:, cols] // INNER
        full = jnp.dot(la[...], oh[:, cols], preferred_element_type=F32)
        out = jnp.zeros((16, WIDTH), F32)
        for m in range(blocks):
            lo = 16 * m
            value = full[lo:lo + 16] + full[rows + lo:rows + lo + 16] + full[2 * rows + lo:2 * rows + lo + 16]
            out = jnp.where(outer == m, value, out)
        return out[:horizon]

    def block_of(m):
        return pl.ds(INNER * m, INNER)

    def region_sum(f, h):
        parts = split3(recv[f, :, h, :])
        return jnp.dot(gather3, jnp.concatenate(parts, axis=0), preferred_element_type=F32)

    def region_spread(f, h, values):
        qs[f, :, h, :] = jnp.dot(spread3, jnp.concatenate(split3(values), axis=0), preferred_element_type=F32)

    def add_moment(k, prod):
        total = prod[:, 0:128]
        for i in range(1, WIDTH // 128):
            total = total + prod[:, 128 * i:128 * (i + 1)]
        mom[k, :, :] += total

    def each_group(before, work, after):
        def step(a, c):
            g = st_of(a)
            before(g)
            def inner(i, d):
                work(columns(g * subs + i, WIDTH))
                return d
            lax.fori_loop(0, subs, inner, 0)
            after(a)
            return c
        lax.fori_loop(0, ns, step, 0)

    nothing = lambda *_: None

    pl.semaphore_wait(barrier, n - 1)
    def first(a, c):
        send_out(0, bb, a)
        return c
    lax.fori_loop(0, ns, first, 0)

    acc[...] = jnp.zeros_like(acc)
    each_group(nothing, lambda cols: category_add(bb[:, cols], cols), nothing)
    for m in range(blocks):
        spread_set(m, wc[:, block_of(m)] * (bc[:, block_of(m)] - category_total(m)))

    def set_p0(cols):
        p0[:, cols] = category_spread(cols)
    each_group(nothing, set_p0, lambda a: send_out(1, p0, a))

    wait_out(0)
    for h in range(horizon):
        b0 = wr[:, h, :] * (br[:, h, :] - region_sum(0, h))
        breg[h, :, :] = b0
        region_spread(0, h, b0)
    send_back(0)
    wait_out(1)
    for h in range(horizon):
        region_spread(1, h, wr[:, h, :] * (region_sum(1, h) + counts * breg[h, :, :]))
    send_back(1)

    acc[...] = jnp.zeros_like(acc)
    def set_v0(cols):
        x = p0[:, cols] + q[0, :, cols]
        v0[:, cols] = x
        add_moment(0, x * x)
        category_add(x, cols)
    each_group(lambda g: wait_back(0, g), set_v0, nothing)

    for m in range(blocks):
        spread_set(m, wc[:, block_of(m)] * category_total(m))
    acc[...] = jnp.zeros_like(acc)
    def set_v1(cols):
        x = v0[:, cols]
        y = wb[:, cols] * x + category_spread(cols) + q[1, :, cols]
        v1[:, cols] = y
        add_moment(1, x * y)
        add_moment(2, y * y)
        category_add(y, cols)
    each_group(lambda g: wait_back(1, g), set_v1, lambda a: send_out(2, v1, a))

    for m in range(blocks):
        spread_set(m, wc[:, block_of(m)] * category_total(m))
    def set_u2(cols):
        u2[:, cols] = wb[:, cols] * v1[:, cols] + category_spread(cols)
    each_group(nothing, set_u2, lambda a: send_out(3, u2, a))

    wait_out(2)
    for h in range(horizon):
        b2 = wr[:, h, :] * region_sum(2, h)
        breg[h, :, :] = b2
        region_spread(2, h, b2)
    send_back(2)
    wait_out(3)
    for h in range(horizon):
        total = region_sum(3, h) + counts * breg[h, :, :]
        b3 = wr[:, h, :] * total
        erow[...] += total * b3
        region_spread(3, h, b3)
    send_back(3)

    acc[...] = jnp.zeros_like(acc)
    def set_v2(cols):
        z = u2[:, cols] + q[2, :, cols]
        tt[:, cols] = z
        add_moment(3, v1[:, cols] * z)
        add_moment(4, z * z)
        add_moment(5, wb[:, cols] * z * z)
        category_add(z, cols)
    each_group(lambda g: wait_back(2, g), set_v2, nothing)

    energy = jnp.zeros((horizon, INNER), F32)
    for m in range(blocks):
        total = category_total(m)
        a3 = wc[:, block_of(m)] * total
        energy = energy + total * a3
        spread_set(m, a3)

    lanes = lax.broadcasted_iota(jnp.int32, (1, 128), 1)
    row = jnp.zeros((1, 128), F32)
    for k in range(6):
        value = jnp.sum(mom[k, :, :], keepdims=True)
        if k == 5:
            value = value + (jnp.sum(energy, keepdims=True) + jnp.sum(erow[...], keepdims=True))
        row = jnp.where(lanes == k, value, row)
    arow[...] = row
    def reduce_send(a, c):
        send_group(a, lambda p: arow, ared.at[me], send_a, recv_a)
        return c
    lax.fori_loop(0, ns, reduce_send, 0)

    def set_rest(cols):
        p0[:, cols] = wb[:, cols] * tt[:, cols] + category_spread(cols)
    pltpu.make_async_copy(recv.at[1, pl.ds(0, n - 1)], recv.at[1, pl.ds(0, n - 1)], send_f.at[1]).wait()
    each_group(nothing, set_rest, nothing)

    pltpu.make_async_copy(ared, ared, recv_a).wait()
    high, low = ared[...], jnp.zeros((n, 1, 128), F32)
    while high.shape[0] > 1:
        half = high.shape[0] // 2
        high, low = pair_add((high[:half], low[:half]), (high[half:], low[half:]))
    high, low = high[0], low[0]
    moments = [(high[:, k:k + 1], low[:, k:k + 1]) for k in range(6)]
    (c1, c2, c3), (e0, e1, e2) = step_coefficients(moments)

    def finish(cols):
        x0, x1, x2 = v0[:, cols], v1[:, cols], tt[:, cols]
        x3 = p0[:, cols] + q[3, :, cols]
        res[:, cols] = x0 + c1 * x1 + c2 * x2 + c3 * x3
        rec[:, cols] = bb[:, cols] + (e0 * x0 + e1 * x1 + e2 * x2)
    each_group(lambda g: wait_back(3, g), finish, nothing)

    for f in (0, 2, 3):
        pltpu.make_async_copy(recv.at[f, pl.ds(0, n - 1)], recv.at[f, pl.ds(0, n - 1)], send_f.at[f]).wait()
    for f in range(4):
        pltpu.make_async_copy(qs.at[f, pl.ds(0, n - 1)], qs.at[f, pl.ds(0, n - 1)], send_q.at[f]).wait()
    pltpu.make_async_copy(ared.at[pl.ds(0, n - 1)], ared.at[pl.ds(0, n - 1)], send_a).wait()


def on_device(ns, nk, bb, wb, bc, wc, br, wr, cm, rm):
    n = ns * nk
    _, horizon, skus = bb.shape
    n_cat = bc.shape[2]
    regions, _, wide = br.shape
    blocks = n_cat // INNER
    vmem = pl.BlockSpec(memory_space=pltpu.VMEM)
    field = jax.ShapeDtypeStruct((horizon, skus), F32)
    rows = 3 * 16 * blocks
    rec, res = pl.pallas_call(
        functools.partial(kernel, ns, nk),
        out_shape=(field, field),
        in_specs=[vmem] * 8,
        out_specs=(vmem, vmem),
        scratch_shapes=[
            pltpu.VMEM((INNER, skus), BF16),
            pltpu.VMEM((rows, WIDTH), BF16),
            pltpu.VMEM((rows, INNER), BF16),
            pltpu.VMEM((rows, INNER), F32),
            *[pltpu.VMEM((horizon, skus), F32)] * 5,
            pltpu.VMEM((4, horizon, skus), F32),
            pltpu.VMEM((4, n, horizon, wide), F32),
            pltpu.VMEM((4, n, horizon, wide), F32),
            pltpu.VMEM((horizon, regions, wide), F32),
            pltpu.VMEM((6, horizon, 128), F32),
            pltpu.VMEM((regions, wide), F32),
            pltpu.VMEM((1, 128), F32),
            pltpu.VMEM((n, 1, 128), F32),
            pltpu.SemaphoreType.DMA((4,)),
            pltpu.SemaphoreType.DMA((4,)),
            pltpu.SemaphoreType.DMA((4,)),
            pltpu.SemaphoreType.DMA((4, ns)),
            pltpu.SemaphoreType.DMA,
            pltpu.SemaphoreType.DMA,
        ],
        compiler_params=pltpu.CompilerParams(
            collective_id=0, has_side_effects=True, vmem_limit_bytes=56 * 2**20
        ),
    )(
        bb.reshape(horizon, skus), wb.reshape(horizon, skus), bc.reshape(horizon, n_cat),
        wc.reshape(horizon, n_cat), br, wr, cm.reshape(1, skus), rm.reshape(1, n),
    )
    return rec.reshape(1, horizon, skus), res.reshape(1, horizon, skus)


def solution(mesh):
    ns, nk = mesh.shape["store"], mesh.shape["sku"]
    split = P(("store", "sku"), None, None)
    by_sku = P(None, None, ("store", "sku"))
    return jax.shard_map(
        functools.partial(on_device, ns, nk), mesh=mesh,
        in_specs=(split, split, split, split, by_sku, by_sku, P(), P()),
        out_specs=(split, split), check_vma=False,
    )
```

```python
import functools

import jax
import jax.numpy as jnp
from jax import lax
from jax.experimental import pallas as pl
from jax.experimental.pallas import tpu as pltpu
from jax.sharding import PartitionSpec as P

MESH = pl.DeviceIdType.MESH
F32, BF16 = jnp.float32, jnp.bfloat16
INNER = 256
WIDTH = 2048


def split3(x):
    hi = x.astype(BF16)
    rest = x - hi.astype(F32)
    mid = rest.astype(BF16)
    low = (rest - mid.astype(F32)).astype(BF16)
    return hi, mid, low


def two_sum(a, b):
    s = a + b
    t = s - a
    return s, (a - (s - t)) + (b - t)


def two_product(a, b):
    p = a * b
    ta, tb = a * 4097.0, b * 4097.0
    ah, bh = ta - (ta - a), tb - (tb - b)
    al, bl = a - ah, b - bh
    return p, ((ah * bh - p) + ah * bl + al * bh) + al * bl


def pair_add(a, b):
    s, e = two_sum(a[0], b[0])
    e = e + (a[1] + b[1])
    high = s + e
    return high, e - (high - s)


def pair_mul(a, b):
    p, e = two_product(a[0], b[0])
    e = e + (a[0] * b[1] + a[1] * b[0])
    high = p + e
    return high, e - (high - p)


def pair_neg(a):
    return -a[0], -a[1]


def pair_div(a, b):
    q1 = a[0] / b[0]
    zero = jnp.zeros_like(q1)
    r = pair_add(a, pair_neg(pair_mul((q1, zero), b)))
    q2 = r[0] / b[0]
    r = pair_add(r, pair_neg(pair_mul((q2, zero), b)))
    q3 = r[0] / b[0]
    high, low = two_sum(q1, q2)
    return pair_add((high, low), (q3, zero))


def step_coefficients(m):
    one = (jnp.ones_like(m[0][0]), jnp.zeros_like(m[0][0]))
    scale = pair_div(m[0], m[1])
    inv = pair_div(one, m[0])
    mu, power = [one, one], scale
    powers = [one, scale]
    for k in range(2, 6):
        power = pair_mul(power, scale)
        powers.append(power)
        mu.append(pair_mul(pair_mul(m[k], inv), power))
    rr1 = pair_add(mu[2], pair_neg(one))
    a1 = pair_div(rr1, pair_add(mu[3], pair_neg(pair_mul(mu[2], mu[2]))))
    g0, g1, g2 = one, pair_neg(pair_add(one, pair_mul(a1, mu[2]))), a1
    rr2 = pair_mul(g2, pair_add(pair_add(mu[2], pair_mul(g1, mu[3])), pair_mul(g2, mu[4])))
    b1 = pair_div(rr2, rr1)
    h0 = pair_add(g0, pair_mul(b1, mu[2]))
    h1 = pair_add(g1, pair_neg(b1))
    h2 = g2
    energy = pair_mul(
        h2, pair_add(pair_add(pair_mul(h0, mu[3]), pair_mul(h1, mu[4])), pair_mul(h2, mu[5]))
    )
    a2 = pair_div(rr2, energy)
    c1 = pair_mul(pair_add(g1, pair_neg(pair_mul(a2, h0))), powers[1])
    c2 = pair_mul(pair_add(g2, pair_neg(pair_mul(a2, h1))), powers[2])
    c3 = pair_mul(pair_neg(pair_mul(a2, h2)), powers[3])
    e0 = pair_mul(pair_add(pair_add(one, pair_mul(a1, mu[2])), pair_mul(a2, h0)), powers[1])
    e1 = pair_mul(pair_add(pair_mul(a2, h1), pair_neg(a1)), powers[2])
    e2 = pair_mul(pair_mul(a2, h2), powers[3])
    return [c[0] for c in (c1, c2, c3)], [e[0] for e in (e0, e1, e2)]


def kernel(
    ns, nk,
    bb_in, wb_in, bc, wc, br, wr, cm, rm,
    rec, res,
    oh, lx, la, acc, bb, wb, p0, v0, v1, u2, tt, q, recv, qs, shape, breg, mom, erow, arow, ared,
    send_f, recv_f, send_q, recv_q, send_a, recv_a,
):
    n = ns * nk
    horizon, skus = bb.shape
    n_cat = bc.shape[0] * 128 // horizon
    _, regions, wide = br.shape
    blocks = n_cat // INNER
    rows = 16 * blocks
    group = nk * wide
    subs = group // WIDTH
    st, sk = lax.axis_index("store"), lax.axis_index("sku")
    me = st * nk + sk

    def flipped(x, count):
        bits = [k for k in range(10) if 2**k < count]
        return [sum((2**k * (1 - 2 * ((x // 2**k) % 2)) for k in bits if (t // 2**k) % 2), x) for t in range(count)]

    sk_of = flipped(sk, nk)

    def st_of(a):
        out = 0
        for k in range(10):
            if 2**k < ns:
                out = out + ((st // 2**k + a // 2**k) % 2) * 2**k
        return out

    barrier = pltpu.get_barrier_semaphore()

    def greet(a, c):
        ps = st_of(a)
        for b in range(nk):
            def one_signal():
                pl.semaphore_signal(barrier, inc=1, device_id=(ps, sk_of[b]), device_id_type=MESH)
            if b == 0:
                pl.when(a > 0)(one_signal)
            else:
                one_signal()
        return c

    lax.fori_loop(0, ns, greet, 0)

    def columns(index, width):
        return pl.ds(pl.multiple_of(index * width, width), width)

    def send_group(a, src_of, dst, send_sem, recv_sem):
        ps = st_of(a)
        for b in range(nk):
            src = src_of(ps * nk + sk_of[b])
            def remote():
                pltpu.make_async_remote_copy(
                    src_ref=src, dst_ref=dst, send_sem=send_sem, recv_sem=recv_sem,
                    device_id=(ps, sk_of[b]), device_id_type=MESH,
                ).start()
            if b == 0:
                pl.when(a > 0)(remote)
                @pl.when(a == 0)
                def _():
                    pltpu.make_async_copy(src, dst, recv_sem).start()
            else:
                remote()

    def slot(p):
        return pl.ds(pl.multiple_of(p * 16, 16), horizon)

    def send_out(f, field, a):
        send_group(a, lambda p: field.at[:, columns(p, wide)], recv.at[f, slot(me)], send_f.at[f], recv_f.at[f])

    def send_back(f):
        def step(a, c):
            send_group(
                a, lambda p: qs.at[f, slot(p)], q.at[f, :, columns(me, wide)], send_q.at[f], recv_q.at[f, st]
            )
            return c
        lax.fori_loop(0, ns, step, 0)

    def wait_out(f):
        pltpu.make_async_copy(shape, shape, recv_f.at[f]).wait()

    def wait_back(f, g):
        part = shape.at[pl.ds(0, nk)]
        pltpu.make_async_copy(part, part, recv_q.at[f, g]).wait()

    def category_add(x, cols):
        outer = cm[:, cols] // INNER
        for piece, part in enumerate(split3(x)):
            part = part.astype(F32)
            for m in range(blocks):
                lx[pl.ds(rows * piece + 16 * m, horizon), :] = jnp.where(outer == m, part, 0.0).astype(BF16)
        acc[...] += lax.dot_general(
            lx[...], oh[:, cols], (((1,), (1,)), ((), ())), preferred_element_type=F32
        )

    def category_total(m):
        return (
            acc[pl.ds(16 * m, horizon), :]
            + acc[pl.ds(rows + 16 * m, horizon), :]
            + acc[pl.ds(2 * rows + 16 * m, horizon), :]
        )

    def spread_set(m, values):
        for piece, part in enumerate(split3(values)):
            la[pl.ds(rows * piece + 16 * m, horizon), :] = part

    def category_spread(cols):
        outer = cm[:, cols] // INNER
        full = jnp.dot(la[...], oh[:, cols], preferred_element_type=F32)
        out = jnp.zeros((16, WIDTH), F32)
        for m in range(blocks):
            lo = 16 * m
            value = full[lo:lo + 16] + full[rows + lo:rows + lo + 16] + full[2 * rows + lo:2 * rows + lo + 16]
            out = jnp.where(outer == m, value, out)
        return out[:horizon]

    def block_of(ref, m):
        tiles = INNER // 128
        return jnp.concatenate(
            [ref[pl.ds(tiles * m + i, horizon, stride=n_cat // 128), :] for i in range(tiles)], axis=1
        )

    def region_sum(f):
        x = jnp.concatenate([recv[f, pl.ds(h, n, stride=16), :] for h in range(horizon)], axis=1)
        return jnp.dot(gather3, jnp.concatenate(split3(x), axis=0), preferred_element_type=F32)

    def region_spread(f, values):
        out = jnp.dot(spread3, jnp.concatenate(split3(values), axis=0), preferred_element_type=F32)
        for h in range(horizon):
            qs[f, pl.ds(h, n, stride=16), :] = out[:, wide * h:wide * (h + 1)]

    def by_horizon(ref):
        return jnp.concatenate([ref[h] for h in range(horizon)], axis=1)

    def add_moment(k, prod):
        total = prod[:, 0:128]
        for i in range(1, WIDTH // 128):
            total = total + prod[:, 128 * i:128 * (i + 1)]
        mom[k, :, :] += total

    def each_group(before, work, after):
        def step(a, c):
            g = st_of(a)
            before(g)
            def inner(i, d):
                work(columns(g * subs + i, WIDTH))
                return d
            lax.fori_loop(0, subs, inner, 0)
            after(a)
            return c
        lax.fori_loop(0, ns, step, 0)

    nothing = lambda *_: None

    def rows_to_tiles(src, dst, tile, total):
        dst[:, columns(tile, 128)] = src[pl.ds(tile, horizon, stride=total), :]

    pl.semaphore_wait(barrier, n - 1)
    def first(a, c):
        g = st_of(a)
        for i in range(group // 128):
            rows_to_tiles(bb_in, bb, g * (group // 128) + i, skus // 128)
        send_out(0, bb, a)
        return c
    lax.fori_loop(0, ns, first, 0)

    def fill(i, c):
        cols = columns(i, WIDTH)
        inner = cm[:, cols] % INNER
        ids = lax.broadcasted_iota(jnp.int32, (INNER, WIDTH), 0)
        oh[:, cols] = jnp.where(ids == inner, 1.0, 0.0).astype(BF16)
        return c

    lax.fori_loop(0, skus // WIDTH, fill, 0)
    lx[...] = jnp.zeros_like(lx)
    la[...] = jnp.zeros_like(la)
    mom[...] = jnp.zeros_like(mom)
    region_hot = jnp.where(lax.broadcasted_iota(jnp.int32, (regions, n), 0) == rm[...], 1.0, 0.0)
    counts = jnp.sum(region_hot, axis=1, keepdims=True)
    gather3 = jnp.concatenate([region_hot.astype(BF16)] * 3, axis=1)
    eye = jnp.where(
        lax.broadcasted_iota(jnp.int32, (n, n), 0) == lax.broadcasted_iota(jnp.int32, (n, n), 1), 1.0, 0.0
    ).astype(BF16)
    spread3 = lax.dot_general(
        eye, jnp.concatenate([region_hot.astype(BF16)] * 3, axis=0), (((1,), (1,)), ((), ())),
        preferred_element_type=F32,
    ).astype(BF16)


    def wb_tiles(i, c):
        for k in range(8):
            rows_to_tiles(wb_in, wb, i * 8 + k, skus // 128)
        return c
    lax.fori_loop(0, skus // 1024, wb_tiles, 0)

    acc[...] = jnp.zeros_like(acc)
    each_group(nothing, lambda cols: category_add(bb[:, cols], cols), nothing)
    for m in range(blocks):
        spread_set(m, block_of(wc, m) * (block_of(bc, m) - category_total(m)))

    def set_p0(cols):
        p0[:, cols] = category_spread(cols)
    each_group(nothing, set_p0, lambda a: send_out(1, p0, a))

    wait_out(0)
    b0 = by_horizon(wr) * (by_horizon(br) - region_sum(0))
    breg[...] = b0
    region_spread(0, b0)
    send_back(0)
    wait_out(1)
    region_spread(1, by_horizon(wr) * (region_sum(1) + counts * breg[...]))
    send_back(1)

    acc[...] = jnp.zeros_like(acc)
    def set_v0(cols):
        x = p0[:, cols] + q[0, :, cols]
        v0[:, cols] = x
        add_moment(0, x * x)
        category_add(x, cols)
    each_group(lambda g: wait_back(0, g), set_v0, nothing)

    for m in range(blocks):
        spread_set(m, block_of(wc, m) * category_total(m))
    acc[...] = jnp.zeros_like(acc)
    def set_v1(cols):
        x = v0[:, cols]
        y = wb[:, cols] * x + category_spread(cols) + q[1, :, cols]
        v1[:, cols] = y
        add_moment(1, x * y)
        add_moment(2, y * y)
        category_add(y, cols)
    each_group(lambda g: wait_back(1, g), set_v1, lambda a: send_out(2, v1, a))

    for m in range(blocks):
        spread_set(m, block_of(wc, m) * category_total(m))
    def set_u2(cols):
        u2[:, cols] = wb[:, cols] * v1[:, cols] + category_spread(cols)
    each_group(nothing, set_u2, lambda a: send_out(3, u2, a))

    wait_out(2)
    b2 = by_horizon(wr) * region_sum(2)
    breg[...] = b2
    region_spread(2, b2)
    send_back(2)
    wait_out(3)
    total3 = region_sum(3) + counts * breg[...]
    b3 = by_horizon(wr) * total3
    erow[...] = total3 * b3
    region_spread(3, b3)
    send_back(3)

    acc[...] = jnp.zeros_like(acc)
    def set_v2(cols):
        z = u2[:, cols] + q[2, :, cols]
        tt[:, cols] = z
        add_moment(3, v1[:, cols] * z)
        add_moment(4, z * z)
        add_moment(5, wb[:, cols] * z * z)
        category_add(z, cols)
    each_group(lambda g: wait_back(2, g), set_v2, nothing)

    energy = jnp.zeros((horizon, INNER), F32)
    for m in range(blocks):
        total = category_total(m)
        a3 = block_of(wc, m) * total
        energy = energy + total * a3
        spread_set(m, a3)

    lanes = lax.broadcasted_iota(jnp.int32, (1, 128), 1)
    row = jnp.zeros((1, 128), F32)
    for k in range(6):
        value = jnp.sum(mom[k, :, :], keepdims=True)
        if k == 5:
            value = value + (jnp.sum(energy, keepdims=True) + jnp.sum(erow[...], keepdims=True))
        row = jnp.where(lanes == k, value, row)
    arow[...] = row
    def reduce_send(a, c):
        send_group(a, lambda p: arow, ared.at[me], send_a, recv_a)
        return c
    lax.fori_loop(0, ns, reduce_send, 0)

    def set_rest(cols):
        p0[:, cols] = wb[:, cols] * tt[:, cols] + category_spread(cols)
    pltpu.make_async_copy(shape.at[pl.ds(0, n - 1)], shape.at[pl.ds(0, n - 1)], send_f.at[1]).wait()
    each_group(nothing, set_rest, nothing)

    pltpu.make_async_copy(ared, ared, recv_a).wait()
    high, low = ared[...], jnp.zeros((n, 1, 128), F32)
    while high.shape[0] > 1:
        half = high.shape[0] // 2
        high, low = pair_add((high[:half], low[:half]), (high[half:], low[half:]))
    high, low = high[0], low[0]
    moments = [(high[:, k:k + 1], low[:, k:k + 1]) for k in range(6)]
    (c1, c2, c3), (e0, e1, e2) = step_coefficients(moments)

    def finish(cols):
        x0, x1, x2 = v0[:, cols], v1[:, cols], tt[:, cols]
        x3 = p0[:, cols] + q[3, :, cols]
        return (x0 + c1 * x1 + c2 * x2 + c3 * x3, bb[:, cols] + (e0 * x0 + e1 * x1 + e2 * x2))

    def finish_group(a, c):
        g = st_of(a)
        wait_back(3, g)
        def inner(i, d):
            first_tile = (g * subs + i) * (WIDTH // 128)
            out_res, out_rec = finish(columns(g * subs + i, WIDTH))
            for k in range(WIDTH // 128):
                at = pl.ds(first_tile + k, horizon, stride=skus // 128)
                res[at, :] = out_res[:, 128 * k:128 * (k + 1)]
                rec[at, :] = out_rec[:, 128 * k:128 * (k + 1)]
            return d
        return lax.fori_loop(0, subs, inner, c)
    lax.fori_loop(0, ns, finish_group, 0)

    for f in (0, 2, 3):
        pltpu.make_async_copy(shape.at[pl.ds(0, n - 1)], shape.at[pl.ds(0, n - 1)], send_f.at[f]).wait()
    for f in range(4):
        pltpu.make_async_copy(shape.at[pl.ds(0, n - 1)], shape.at[pl.ds(0, n - 1)], send_q.at[f]).wait()
    pltpu.make_async_copy(ared.at[pl.ds(0, n - 1)], ared.at[pl.ds(0, n - 1)], send_a).wait()


def on_device(ns, nk, bb, wb, bc, wc, br, wr, cm, rm):
    n = ns * nk
    _, horizon, skus = bb.shape
    n_cat = bc.shape[2]
    regions, _, wide = br.shape
    blocks = n_cat // INNER
    vmem = pl.BlockSpec(memory_space=pltpu.VMEM)
    field = jax.ShapeDtypeStruct((horizon * skus // 128, 128), F32)
    rows = 3 * 16 * blocks
    rec, res = pl.pallas_call(
        functools.partial(kernel, ns, nk),
        out_shape=(field, field),
        in_specs=[vmem] * 8,
        out_specs=(vmem, vmem),
        scratch_shapes=[
            pltpu.VMEM((INNER, skus), BF16),
            pltpu.VMEM((rows, WIDTH), BF16),
            pltpu.VMEM((rows, INNER), BF16),
            pltpu.VMEM((rows, INNER), F32),
            *[pltpu.VMEM((horizon, skus), F32)] * 7,
            pltpu.VMEM((4, horizon, skus), F32),
            pltpu.VMEM((4, n * 16, wide), F32),
            pltpu.VMEM((4, n * 16, wide), F32),
            pltpu.VMEM((n, horizon, wide), F32),
            pltpu.VMEM((regions, horizon * wide), F32),
            pltpu.VMEM((6, horizon, 128), F32),
            pltpu.VMEM((regions, horizon * wide), F32),
            pltpu.VMEM((1, 128), F32),
            pltpu.VMEM((n, 1, 128), F32),
            pltpu.SemaphoreType.DMA((4,)),
            pltpu.SemaphoreType.DMA((4,)),
            pltpu.SemaphoreType.DMA((4,)),
            pltpu.SemaphoreType.DMA((4, ns)),
            pltpu.SemaphoreType.DMA,
            pltpu.SemaphoreType.DMA,
        ],
        compiler_params=pltpu.CompilerParams(
            collective_id=0, has_side_effects=True, vmem_limit_bytes=56 * 2**20
        ),
    )(
        bb.reshape(-1, 128), wb.reshape(-1, 128), bc.reshape(-1, 128), wc.reshape(-1, 128),
        br.transpose(1, 0, 2), wr.transpose(1, 0, 2), cm.reshape(1, skus), rm.reshape(1, n),
    )
    return rec.reshape(1, horizon, skus), res.reshape(1, horizon, skus)


def solution(mesh):
    ns, nk = mesh.shape["store"], mesh.shape["sku"]
    split = P(("store", "sku"), None, None)
    by_sku = P(None, None, ("store", "sku"))
    return jax.shard_map(
        functools.partial(on_device, ns, nk), mesh=mesh,
        in_specs=(split, split, split, split, by_sku, by_sku, P(), P()),
        out_specs=(split, split), check_vma=False,
    )
```

```python
import functools

import jax
import jax.numpy as jnp
from jax import lax
from jax.experimental import pallas as pl
from jax.experimental.pallas import tpu as pltpu
from jax.sharding import PartitionSpec as P

MESH = pl.DeviceIdType.MESH
F32, BF16 = jnp.float32, jnp.bfloat16
INNER = 256
WIDTH = 2048


def split3(x):
    hi = x.astype(BF16)
    rest = x - hi.astype(F32)
    mid = rest.astype(BF16)
    low = (rest - mid.astype(F32)).astype(BF16)
    return hi, mid, low


def two_sum(a, b):
    s = a + b
    t = s - a
    return s, (a - (s - t)) + (b - t)


def two_product(a, b):
    p = a * b
    ta, tb = a * 4097.0, b * 4097.0
    ah, bh = ta - (ta - a), tb - (tb - b)
    al, bl = a - ah, b - bh
    return p, ((ah * bh - p) + ah * bl + al * bh) + al * bl


def pair_add(a, b):
    s, e = two_sum(a[0], b[0])
    e = e + (a[1] + b[1])
    high = s + e
    return high, e - (high - s)


def pair_mul(a, b):
    p, e = two_product(a[0], b[0])
    e = e + (a[0] * b[1] + a[1] * b[0])
    high = p + e
    return high, e - (high - p)


def pair_neg(a):
    return -a[0], -a[1]


def pair_div(a, b):
    q1 = a[0] / b[0]
    zero = jnp.zeros_like(q1)
    r = pair_add(a, pair_neg(pair_mul((q1, zero), b)))
    q2 = r[0] / b[0]
    r = pair_add(r, pair_neg(pair_mul((q2, zero), b)))
    q3 = r[0] / b[0]
    high, low = two_sum(q1, q2)
    return pair_add((high, low), (q3, zero))


def step_coefficients(m):
    one = (jnp.ones_like(m[0][0]), jnp.zeros_like(m[0][0]))
    scale = pair_div(m[0], m[1])
    inv = pair_div(one, m[0])
    mu, power = [one, one], scale
    powers = [one, scale]
    for k in range(2, 6):
        power = pair_mul(power, scale)
        powers.append(power)
        mu.append(pair_mul(pair_mul(m[k], inv), power))
    rr1 = pair_add(mu[2], pair_neg(one))
    a1 = pair_div(rr1, pair_add(mu[3], pair_neg(pair_mul(mu[2], mu[2]))))
    g0, g1, g2 = one, pair_neg(pair_add(one, pair_mul(a1, mu[2]))), a1
    rr2 = pair_mul(g2, pair_add(pair_add(mu[2], pair_mul(g1, mu[3])), pair_mul(g2, mu[4])))
    b1 = pair_div(rr2, rr1)
    h0 = pair_add(g0, pair_mul(b1, mu[2]))
    h1 = pair_add(g1, pair_neg(b1))
    h2 = g2
    energy = pair_mul(
        h2, pair_add(pair_add(pair_mul(h0, mu[3]), pair_mul(h1, mu[4])), pair_mul(h2, mu[5]))
    )
    a2 = pair_div(rr2, energy)
    c1 = pair_mul(pair_add(g1, pair_neg(pair_mul(a2, h0))), powers[1])
    c2 = pair_mul(pair_add(g2, pair_neg(pair_mul(a2, h1))), powers[2])
    c3 = pair_mul(pair_neg(pair_mul(a2, h2)), powers[3])
    e0 = pair_mul(pair_add(pair_add(one, pair_mul(a1, mu[2])), pair_mul(a2, h0)), powers[1])
    e1 = pair_mul(pair_add(pair_mul(a2, h1), pair_neg(a1)), powers[2])
    e2 = pair_mul(pair_mul(a2, h2), powers[3])
    return [c[0] for c in (c1, c2, c3)], [e[0] for e in (e0, e1, e2)]


def kernel(
    ns, nk,
    bb_hbm, wb_hbm, bc_hbm, wc_hbm, br_hbm, wr_hbm, cm, rm,
    rec, res,
    bb_in, wb_in, bc, wc, br, wr, oh, lx, la, acc, bb, wb, p0, v0, u1, v1, u2, tt, q, recv, qs, shape, breg, mom, erow, arow, ared,
    send_f, recv_f, send_q, recv_q, send_a, recv_a, load,
):
    n = ns * nk
    horizon, skus = bb.shape
    n_cat = bc.shape[0] * 128 // horizon
    _, regions, wide = br.shape
    blocks = n_cat // INNER
    rows = 16 * blocks
    group = nk * wide
    subs = group // WIDTH
    st, sk = lax.axis_index("store"), lax.axis_index("sku")
    me = st * nk + sk

    def flipped(x, count):
        bits = [k for k in range(10) if 2**k < count]
        return [sum((2**k * (1 - 2 * ((x // 2**k) % 2)) for k in bits if (t // 2**k) % 2), x) for t in range(count)]

    sk_of = flipped(sk, nk)

    def st_of(a):
        out = 0
        for k in range(10):
            if 2**k < ns:
                out = out + ((st // 2**k + a // 2**k) % 2) * 2**k
        return out

    loads = [
        pltpu.make_async_copy(src, dst, load.at[i])
        for i, (src, dst) in enumerate(
            [(bb_hbm, bb_in), (bc_hbm, bc), (wc_hbm, wc), (br_hbm, br), (wr_hbm, wr), (wb_hbm, wb_in)]
        )
    ]
    for one in loads:
        one.start()
    barrier = pltpu.get_barrier_semaphore()

    def greet(a, c):
        ps = st_of(a)
        for b in range(nk):
            def one_signal():
                pl.semaphore_signal(barrier, inc=1, device_id=(ps, sk_of[b]), device_id_type=MESH)
            if b == 0:
                pl.when(a > 0)(one_signal)
            else:
                one_signal()
        return c

    lax.fori_loop(0, ns, greet, 0)

    def columns(index, width):
        return pl.ds(pl.multiple_of(index * width, width), width)

    def send_group(a, src_of, dst, send_sem, recv_sem):
        ps = st_of(a)
        for b in range(nk):
            src = src_of(ps * nk + sk_of[b])
            def remote():
                pltpu.make_async_remote_copy(
                    src_ref=src, dst_ref=dst, send_sem=send_sem, recv_sem=recv_sem,
                    device_id=(ps, sk_of[b]), device_id_type=MESH,
                ).start()
            if b == 0:
                pl.when(a > 0)(remote)
                @pl.when(a == 0)
                def _():
                    pltpu.make_async_copy(src, dst, recv_sem).start()
            else:
                remote()

    def slot(p):
        return pl.ds(pl.multiple_of(p * 16, 16), horizon)

    def send_out(f, field, a):
        send_group(a, lambda p: field.at[:, columns(p, wide)], recv.at[f, slot(me)], send_f.at[f], recv_f.at[f])

    def send_back(f):
        def step(a, c):
            send_group(
                a, lambda p: qs.at[f, slot(p)], q.at[f, :, columns(me, wide)], send_q.at[f], recv_q.at[f, st]
            )
            return c
        lax.fori_loop(0, ns, step, 0)

    def wait_out(f):
        pltpu.make_async_copy(shape, shape, recv_f.at[f]).wait()

    def wait_back(f, g):
        part = shape.at[pl.ds(0, nk)]
        pltpu.make_async_copy(part, part, recv_q.at[f, g]).wait()

    def category_add(x, cols):
        outer = cm[:, cols] // INNER
        for piece, part in enumerate(split3(x)):
            part = part.astype(F32)
            for m in range(blocks):
                lx[pl.ds(rows * piece + 16 * m, horizon), :] = jnp.where(outer == m, part, 0.0).astype(BF16)
        acc[...] += lax.dot_general(
            lx[...], oh[:, cols], (((1,), (1,)), ((), ())), preferred_element_type=F32
        )

    def category_total(m):
        return (
            acc[pl.ds(16 * m, horizon), :]
            + acc[pl.ds(rows + 16 * m, horizon), :]
            + acc[pl.ds(2 * rows + 16 * m, horizon), :]
        )

    def spread_set(m, values):
        for piece, part in enumerate(split3(values)):
            la[pl.ds(rows * piece + 16 * m, horizon), :] = part

    def category_spread(cols):
        outer = cm[:, cols] // INNER
        full = jnp.dot(la[...], oh[:, cols], preferred_element_type=F32)
        out = jnp.zeros((16, WIDTH), F32)
        for m in range(blocks):
            lo = 16 * m
            value = full[lo:lo + 16] + full[rows + lo:rows + lo + 16] + full[2 * rows + lo:2 * rows + lo + 16]
            out = jnp.where(outer == m, value, out)
        return out[:horizon]

    def block_of(ref, m):
        tiles = INNER // 128
        return jnp.concatenate(
            [ref[pl.ds(tiles * m + i, horizon, stride=n_cat // 128), :] for i in range(tiles)], axis=1
        )

    def region_sum(f):
        x = jnp.concatenate([recv[f, pl.ds(h, n, stride=16), :] for h in range(horizon)], axis=1)
        return jnp.dot(gather3, jnp.concatenate(split3(x), axis=0), preferred_element_type=F32)

    def region_spread(f, values):
        out = jnp.dot(spread3, jnp.concatenate(split3(values), axis=0), preferred_element_type=F32)
        for h in range(horizon):
            qs[f, pl.ds(h, n, stride=16), :] = out[:, wide * h:wide * (h + 1)]

    def by_horizon(ref):
        return jnp.concatenate([ref[h] for h in range(horizon)], axis=1)

    def add_moment(k, prod):
        total = prod[:, 0:128]
        for i in range(1, WIDTH // 128):
            total = total + prod[:, 128 * i:128 * (i + 1)]
        mom[k, :, :] += total

    def each_group(before, work, after):
        def step(a, c):
            g = st_of(a)
            before(g)
            def inner(i, d):
                work(columns(g * subs + i, WIDTH))
                return d
            lax.fori_loop(0, subs, inner, 0)
            after(a)
            return c
        lax.fori_loop(0, ns, step, 0)

    nothing = lambda *_: None

    def rows_to_tiles(src, dst, tile, total):
        dst[:, columns(tile, 128)] = src[pl.ds(tile, horizon, stride=total), :]

    loads[0].wait()
    pl.semaphore_wait(barrier, n - 1)
    def first(a, c):
        g = st_of(a)
        for i in range(group // 128):
            rows_to_tiles(bb_in, bb, g * (group // 128) + i, skus // 128)
        send_out(0, bb, a)
        return c
    lax.fori_loop(0, ns, first, 0)

    def fill(i, c):
        cols = columns(i, WIDTH)
        inner = cm[:, cols] % INNER
        ids = lax.broadcasted_iota(jnp.int32, (INNER, WIDTH), 0)
        oh[:, cols] = jnp.where(ids == inner, 1.0, 0.0).astype(BF16)
        return c

    lax.fori_loop(0, skus // WIDTH, fill, 0)
    lx[...] = jnp.zeros_like(lx)
    la[...] = jnp.zeros_like(la)
    mom[...] = jnp.zeros_like(mom)
    region_hot = jnp.where(lax.broadcasted_iota(jnp.int32, (regions, n), 0) == rm[...], 1.0, 0.0)
    counts = jnp.sum(region_hot, axis=1, keepdims=True)
    gather3 = jnp.concatenate([region_hot.astype(BF16)] * 3, axis=1)
    eye = jnp.where(
        lax.broadcasted_iota(jnp.int32, (n, n), 0) == lax.broadcasted_iota(jnp.int32, (n, n), 1), 1.0, 0.0
    ).astype(BF16)
    spread3 = lax.dot_general(
        eye, jnp.concatenate([region_hot.astype(BF16)] * 3, axis=0), (((1,), (1,)), ((), ())),
        preferred_element_type=F32,
    ).astype(BF16)


    for one in loads[1:]:
        one.wait()
    def wb_tiles(i, c):
        for k in range(8):
            rows_to_tiles(wb_in, wb, i * 8 + k, skus // 128)
        return c
    lax.fori_loop(0, skus // 1024, wb_tiles, 0)

    acc[...] = jnp.zeros_like(acc)
    each_group(nothing, lambda cols: category_add(bb[:, cols], cols), nothing)
    for m in range(blocks):
        spread_set(m, block_of(wc, m) * (block_of(bc, m) - category_total(m)))

    def set_p0(cols):
        p0[:, cols] = category_spread(cols)
    each_group(nothing, set_p0, lambda a: send_out(1, p0, a))

    wait_out(0)
    b0 = by_horizon(wr) * (by_horizon(br) - region_sum(0))
    breg[0] = b0
    region_spread(0, b0)
    send_back(0)
    wait_out(1)
    b1 = by_horizon(wr) * (region_sum(1) + counts * breg[0])
    breg[1] = b1
    region_spread(1, b1)
    send_back(1)

    acc[...] = jnp.zeros_like(acc)
    def set_v0(cols):
        x = p0[:, cols] + q[0, :, cols]
        v0[:, cols] = x
        add_moment(0, x * x)
        category_add(x, cols)
    each_group(lambda g: wait_back(0, g), set_v0, nothing)

    for m in range(blocks):
        spread_set(m, block_of(wc, m) * category_total(m))
    def set_u1(cols):
        u1[:, cols] = wb[:, cols] * v0[:, cols] + category_spread(cols)
    each_group(nothing, set_u1, lambda a: send_out(2, u1, a))

    acc[...] = jnp.zeros_like(acc)
    def set_v1(cols):
        y = u1[:, cols] + q[1, :, cols]
        v1[:, cols] = y
        add_moment(1, v0[:, cols] * y)
        add_moment(2, y * y)
        category_add(y, cols)
    each_group(lambda g: wait_back(1, g), set_v1, nothing)

    for m in range(blocks):
        spread_set(m, block_of(wc, m) * category_total(m))
    def set_u2(cols):
        u2[:, cols] = wb[:, cols] * v1[:, cols] + category_spread(cols)
    each_group(nothing, set_u2, lambda a: send_out(3, u2, a))

    wait_out(2)
    b2 = by_horizon(wr) * (region_sum(2) + counts * breg[1])
    breg[0] = b2
    region_spread(2, b2)
    send_back(2)
    wait_out(3)
    total3 = region_sum(3) + counts * breg[0]
    b3 = by_horizon(wr) * total3
    erow[...] = total3 * b3
    region_spread(3, b3)
    send_back(3)

    acc[...] = jnp.zeros_like(acc)
    def set_v2(cols):
        z = u2[:, cols] + q[2, :, cols]
        tt[:, cols] = z
        add_moment(3, v1[:, cols] * z)
        add_moment(4, z * z)
        add_moment(5, wb[:, cols] * z * z)
        category_add(z, cols)
    each_group(lambda g: wait_back(2, g), set_v2, nothing)

    energy = jnp.zeros((horizon, INNER), F32)
    for m in range(blocks):
        total = category_total(m)
        a3 = block_of(wc, m) * total
        energy = energy + total * a3
        spread_set(m, a3)

    lanes = lax.broadcasted_iota(jnp.int32, (1, 128), 1)
    row = jnp.zeros((1, 128), F32)
    for k in range(6):
        value = jnp.sum(mom[k, :, :], keepdims=True)
        if k == 5:
            value = value + (jnp.sum(energy, keepdims=True) + jnp.sum(erow[...], keepdims=True))
        row = jnp.where(lanes == k, value, row)
    arow[...] = row
    def reduce_send(a, c):
        send_group(a, lambda p: arow, ared.at[me], send_a, recv_a)
        return c
    lax.fori_loop(0, ns, reduce_send, 0)

    def set_rest(cols):
        p0[:, cols] = wb[:, cols] * tt[:, cols] + category_spread(cols)
    pltpu.make_async_copy(shape.at[pl.ds(0, n - 1)], shape.at[pl.ds(0, n - 1)], send_f.at[1]).wait()
    each_group(nothing, set_rest, nothing)

    pltpu.make_async_copy(ared, ared, recv_a).wait()
    high, low = ared[...], jnp.zeros((n, 1, 128), F32)
    while high.shape[0] > 1:
        half = high.shape[0] // 2
        high, low = pair_add((high[:half], low[:half]), (high[half:], low[half:]))
    high, low = high[0], low[0]
    moments = [(high[:, k:k + 1], low[:, k:k + 1]) for k in range(6)]
    (c1, c2, c3), (e0, e1, e2) = step_coefficients(moments)

    def finish(cols):
        x0, x1, x2 = v0[:, cols], v1[:, cols], tt[:, cols]
        x3 = p0[:, cols] + q[3, :, cols]
        return (x0 + c1 * x1 + c2 * x2 + c3 * x3, bb[:, cols] + (e0 * x0 + e1 * x1 + e2 * x2))

    def finish_group(a, c):
        g = st_of(a)
        wait_back(3, g)
        def inner(i, d):
            first_tile = (g * subs + i) * (WIDTH // 128)
            out_res, out_rec = finish(columns(g * subs + i, WIDTH))
            for k in range(WIDTH // 128):
                at = pl.ds(first_tile + k, horizon, stride=skus // 128)
                res[at, :] = out_res[:, 128 * k:128 * (k + 1)]
                rec[at, :] = out_rec[:, 128 * k:128 * (k + 1)]
            return d
        return lax.fori_loop(0, subs, inner, c)
    lax.fori_loop(0, ns, finish_group, 0)

    for f in (0, 2, 3):
        pltpu.make_async_copy(shape.at[pl.ds(0, n - 1)], shape.at[pl.ds(0, n - 1)], send_f.at[f]).wait()
    for f in range(4):
        pltpu.make_async_copy(shape.at[pl.ds(0, n - 1)], shape.at[pl.ds(0, n - 1)], send_q.at[f]).wait()
    pltpu.make_async_copy(ared.at[pl.ds(0, n - 1)], ared.at[pl.ds(0, n - 1)], send_a).wait()


def on_device(ns, nk, bb, wb, bc, wc, br, wr, cm, rm):
    n = ns * nk
    _, horizon, skus = bb.shape
    n_cat = bc.shape[2]
    regions, _, wide = br.shape
    blocks = n_cat // INNER
    vmem = pl.BlockSpec(memory_space=pltpu.VMEM)
    field = jax.ShapeDtypeStruct((horizon * skus // 128, 128), F32)
    rows = 3 * 16 * blocks
    rec, res = pl.pallas_call(
        functools.partial(kernel, ns, nk),
        out_shape=(field, field),
        in_specs=[pl.BlockSpec(memory_space=pltpu.HBM)] * 6 + [vmem] * 2,
        out_specs=(vmem, vmem),
        scratch_shapes=[
            *[pltpu.VMEM((horizon * skus // 128, 128), F32)] * 2,
            *[pltpu.VMEM((horizon * n_cat // 128, 128), F32)] * 2,
            *[pltpu.VMEM((horizon, regions, wide), F32)] * 2,
            pltpu.VMEM((INNER, skus), BF16),
            pltpu.VMEM((rows, WIDTH), BF16),
            pltpu.VMEM((rows, INNER), BF16),
            pltpu.VMEM((rows, INNER), F32),
            *[pltpu.VMEM((horizon, skus), F32)] * 8,
            pltpu.VMEM((4, horizon, skus), F32),
            pltpu.VMEM((4, n * 16, wide), F32),
            pltpu.VMEM((4, n * 16, wide), F32),
            pltpu.VMEM((n, horizon, wide), F32),
            pltpu.VMEM((2, regions, horizon * wide), F32),
            pltpu.VMEM((6, horizon, 128), F32),
            pltpu.VMEM((regions, horizon * wide), F32),
            pltpu.VMEM((1, 128), F32),
            pltpu.VMEM((n, 1, 128), F32),
            pltpu.SemaphoreType.DMA((4,)),
            pltpu.SemaphoreType.DMA((4,)),
            pltpu.SemaphoreType.DMA((4,)),
            pltpu.SemaphoreType.DMA((4, ns)),
            pltpu.SemaphoreType.DMA,
            pltpu.SemaphoreType.DMA,
            pltpu.SemaphoreType.DMA((6,)),
        ],
        compiler_params=pltpu.CompilerParams(
            collective_id=0, has_side_effects=True, vmem_limit_bytes=56 * 2**20
        ),
    )(
        bb.reshape(-1, 128), wb.reshape(-1, 128), bc.reshape(-1, 128), wc.reshape(-1, 128),
        br.transpose(1, 0, 2), wr.transpose(1, 0, 2), cm.reshape(1, skus), rm.reshape(1, n),
    )
    return rec.reshape(1, horizon, skus), res.reshape(1, horizon, skus)


def solution(mesh):
    ns, nk = mesh.shape["store"], mesh.shape["sku"]
    split = P(("store", "sku"), None, None)
    by_sku = P(None, None, ("store", "sku"))
    return jax.shard_map(
        functools.partial(on_device, ns, nk), mesh=mesh,
        in_specs=(split, split, split, split, by_sku, by_sku, P(), P()),
        out_specs=(split, split), check_vma=False,
    )
```

```python
import functools

import jax
import jax.numpy as jnp
from jax import lax
from jax.experimental import pallas as pl
from jax.experimental.pallas import tpu as pltpu
from jax.sharding import PartitionSpec as P

MESH = pl.DeviceIdType.MESH
F32, BF16 = jnp.float32, jnp.bfloat16
INNER = 256
PARTS = 4
WIDTH = 2048


def split3(x):
    hi = x.astype(BF16)
    rest = x - hi.astype(F32)
    mid = rest.astype(BF16)
    low = (rest - mid.astype(F32)).astype(BF16)
    return hi, mid, low


def two_sum(a, b):
    s = a + b
    t = s - a
    return s, (a - (s - t)) + (b - t)


def two_product(a, b):
    p = a * b
    ta, tb = a * 4097.0, b * 4097.0
    ah, bh = ta - (ta - a), tb - (tb - b)
    al, bl = a - ah, b - bh
    return p, ((ah * bh - p) + ah * bl + al * bh) + al * bl


def pair_add(a, b):
    s, e = two_sum(a[0], b[0])
    e = e + (a[1] + b[1])
    high = s + e
    return high, e - (high - s)


def pair_mul(a, b):
    p, e = two_product(a[0], b[0])
    e = e + (a[0] * b[1] + a[1] * b[0])
    high = p + e
    return high, e - (high - p)


def pair_neg(a):
    return -a[0], -a[1]


def pair_div(a, b):
    q1 = a[0] / b[0]
    zero = jnp.zeros_like(q1)
    r = pair_add(a, pair_neg(pair_mul((q1, zero), b)))
    q2 = r[0] / b[0]
    r = pair_add(r, pair_neg(pair_mul((q2, zero), b)))
    q3 = r[0] / b[0]
    high, low = two_sum(q1, q2)
    return pair_add((high, low), (q3, zero))


def step_coefficients(m):
    one = (jnp.ones_like(m[0][0]), jnp.zeros_like(m[0][0]))
    scale = pair_div(m[0], m[1])
    inv = pair_div(one, m[0])
    mu, power = [one, one], scale
    powers = [one, scale]
    for k in range(2, 6):
        power = pair_mul(power, scale)
        powers.append(power)
        mu.append(pair_mul(pair_mul(m[k], inv), power))
    rr1 = pair_add(mu[2], pair_neg(one))
    a1 = pair_div(rr1, pair_add(mu[3], pair_neg(pair_mul(mu[2], mu[2]))))
    g0, g1, g2 = one, pair_neg(pair_add(one, pair_mul(a1, mu[2]))), a1
    rr2 = pair_mul(g2, pair_add(pair_add(mu[2], pair_mul(g1, mu[3])), pair_mul(g2, mu[4])))
    b1 = pair_div(rr2, rr1)
    h0 = pair_add(g0, pair_mul(b1, mu[2]))
    h1 = pair_add(g1, pair_neg(b1))
    h2 = g2
    energy = pair_mul(
        h2, pair_add(pair_add(pair_mul(h0, mu[3]), pair_mul(h1, mu[4])), pair_mul(h2, mu[5]))
    )
    a2 = pair_div(rr2, energy)
    c1 = pair_mul(pair_add(g1, pair_neg(pair_mul(a2, h0))), powers[1])
    c2 = pair_mul(pair_add(g2, pair_neg(pair_mul(a2, h1))), powers[2])
    c3 = pair_mul(pair_neg(pair_mul(a2, h2)), powers[3])
    e0 = pair_mul(pair_add(pair_add(one, pair_mul(a1, mu[2])), pair_mul(a2, h0)), powers[1])
    e1 = pair_mul(pair_add(pair_mul(a2, h1), pair_neg(a1)), powers[2])
    e2 = pair_mul(pair_mul(a2, h2), powers[3])
    return [c[0] for c in (c1, c2, c3)], [e[0] for e in (e0, e1, e2)]


def kernel(
    ns, nk,
    bb_hbm, wb_hbm, bc_hbm, wc_hbm, br_hbm, wr_hbm, cm, rm,
    rec, res,
    bb_in, wb_in, bc, wc, br, wr, oh, lx, la, acc, bb, wb, p0, v0, u1, v1, u2, tt, q, recv, qs, shape, breg, mom, erow, arow, ared,
    send_f, recv_f, send_q, recv_q, send_a, recv_a, load,
):
    n = ns * nk
    horizon, skus = bb.shape
    n_cat = bc.shape[0] * 128 // horizon
    _, regions, wide = br.shape
    blocks = n_cat // INNER
    rows = 16 * blocks
    group = nk * wide
    subs = group // WIDTH
    st, sk = lax.axis_index("store"), lax.axis_index("sku")
    me = st * nk + sk

    def flipped(x, count):
        bits = [k for k in range(10) if 2**k < count]
        return [sum((2**k * (1 - 2 * ((x // 2**k) % 2)) for k in bits if (t // 2**k) % 2), x) for t in range(count)]

    sk_of = flipped(sk, nk)

    def st_of(a):
        out = 0
        for k in range(10):
            if 2**k < ns:
                out = out + ((st // 2**k + a // 2**k) % 2) * 2**k
        return out

    loads = [
        pltpu.make_async_copy(src, dst, load.at[i])
        for i, (src, dst) in enumerate(
            [(bb_hbm, bb_in), (bc_hbm, bc), (wc_hbm, wc), (br_hbm, br), (wr_hbm, wr), (wb_hbm, wb_in)]
        )
    ]
    for one in loads:
        one.start()
    barrier = pltpu.get_barrier_semaphore()

    def greet(a, c):
        ps = st_of(a)
        for b in range(nk):
            def one_signal():
                pl.semaphore_signal(barrier, inc=1, device_id=(ps, sk_of[b]), device_id_type=MESH)
            if b == 0:
                pl.when(a > 0)(one_signal)
            else:
                one_signal()
        return c

    lax.fori_loop(0, ns, greet, 0)

    def columns(index, width):
        return pl.ds(pl.multiple_of(index * width, width), width)

    def send_group(a, src_of, dst, send_sem, recv_sem):
        ps = st_of(a)
        for b in range(nk):
            src = src_of(ps * nk + sk_of[b])
            def remote():
                pltpu.make_async_remote_copy(
                    src_ref=src, dst_ref=dst, send_sem=send_sem, recv_sem=recv_sem,
                    device_id=(ps, sk_of[b]), device_id_type=MESH,
                ).start()
            if b == 0:
                pl.when(a > 0)(remote)
                @pl.when(a == 0)
                def _():
                    pltpu.make_async_copy(src, dst, recv_sem).start()
            else:
                remote()

    def slot(p):
        return pl.ds(pl.multiple_of(p * 16, 16), horizon)

    def send_out(f, field, a):
        send_group(a, lambda p: field.at[:, columns(p, wide)], recv.at[f, slot(me)], send_f.at[f], recv_f.at[f])

    def send_back(f):
        def step(a, c):
            send_group(
                a, lambda p: qs.at[f, slot(p)], q.at[f, :, columns(me, wide)], send_q.at[f], recv_q.at[f, st]
            )
            return c
        lax.fori_loop(0, ns, step, 0)

    def wait_out(f):
        pltpu.make_async_copy(shape, shape, recv_f.at[f]).wait()

    def wait_back(f, g):
        part = shape.at[pl.ds(0, nk)]
        pltpu.make_async_copy(part, part, recv_q.at[f, g]).wait()

    def category_add(x, cols):
        outer = cm[:, cols] // INNER
        for piece, part in enumerate(split3(x)):
            part = part.astype(F32)
            for m in range(blocks):
                lx[pl.ds(rows * piece + 16 * m, horizon), :] = jnp.where(outer == m, part, 0.0).astype(BF16)
        acc[...] += lax.dot_general(
            lx[...], oh[:, cols], (((1,), (1,)), ((), ())), preferred_element_type=F32
        )

    def category_total(m):
        return (
            acc[pl.ds(16 * m, horizon), :]
            + acc[pl.ds(rows + 16 * m, horizon), :]
            + acc[pl.ds(2 * rows + 16 * m, horizon), :]
        )

    def spread_set(m, values):
        for piece, part in enumerate(split3(values)):
            la[pl.ds(rows * piece + 16 * m, horizon), :] = part

    def category_spread(cols):
        outer = cm[:, cols] // INNER
        full = jnp.dot(la[...], oh[:, cols], preferred_element_type=F32)
        out = jnp.zeros((16, WIDTH), F32)
        for m in range(blocks):
            lo = 16 * m
            value = full[lo:lo + 16] + full[rows + lo:rows + lo + 16] + full[2 * rows + lo:2 * rows + lo + 16]
            out = jnp.where(outer == m, value, out)
        return out[:horizon]

    def block_of(ref, m):
        tiles = INNER // 128
        return jnp.concatenate(
            [ref[pl.ds(tiles * m + i, horizon, stride=n_cat // 128), :] for i in range(tiles)], axis=1
        )

    def region_sum(f):
        x = jnp.concatenate([recv[f, pl.ds(h, n, stride=16), :] for h in range(horizon)], axis=1)
        return jnp.dot(gather3, jnp.concatenate(split3(x), axis=0), preferred_element_type=F32)

    def region_spread(f, values):
        out = jnp.dot(spread3, jnp.concatenate(split3(values), axis=0), preferred_element_type=F32)
        for h in range(horizon):
            qs[f, pl.ds(h, n, stride=16), :] = out[:, wide * h:wide * (h + 1)]

    def by_horizon(ref):
        return jnp.concatenate([ref[h] for h in range(horizon)], axis=1)

    def add_moment(k, prod):
        total = prod[:, 0:128]
        for i in range(1, WIDTH // 128):
            total = total + prod[:, 128 * i:128 * (i + 1)]
        mom[k, :, :] += total

    def each_group(before, work, after):
        def step(a, c):
            g = st_of(a)
            before(g)
            def inner(i, d):
                work(columns(g * subs + i, WIDTH))
                return d
            lax.fori_loop(0, subs, inner, 0)
            after(a)
            return c
        lax.fori_loop(0, ns, step, 0)

    nothing = lambda *_: None

    def rows_to_tiles(src, dst, tile, total):
        dst[:, columns(tile, 128)] = src[pl.ds(tile, horizon, stride=total), :]

    loads[0].wait()
    pl.semaphore_wait(barrier, n - 1)
    def first(a, c):
        g = st_of(a)
        for i in range(group // 128):
            rows_to_tiles(bb_in, bb, g * (group // 128) + i, skus // 128)
        send_out(0, bb, a)
        return c
    lax.fori_loop(0, ns, first, 0)

    def fill(i, c):
        cols = columns(i, WIDTH)
        inner = cm[:, cols] % INNER
        ids = lax.broadcasted_iota(jnp.int32, (INNER, WIDTH), 0)
        oh[:, cols] = jnp.where(ids == inner, 1.0, 0.0).astype(BF16)
        return c

    lax.fori_loop(0, skus // WIDTH, fill, 0)
    lx[...] = jnp.zeros_like(lx)
    la[...] = jnp.zeros_like(la)
    mom[...] = jnp.zeros_like(mom)
    region_hot = jnp.where(lax.broadcasted_iota(jnp.int32, (regions, n), 0) == rm[...], 1.0, 0.0)
    counts = jnp.sum(region_hot, axis=1, keepdims=True)
    gather3 = jnp.concatenate([region_hot.astype(BF16)] * 3, axis=1)
    eye = jnp.where(
        lax.broadcasted_iota(jnp.int32, (n, n), 0) == lax.broadcasted_iota(jnp.int32, (n, n), 1), 1.0, 0.0
    ).astype(BF16)
    spread3 = lax.dot_general(
        eye, jnp.concatenate([region_hot.astype(BF16)] * 3, axis=0), (((1,), (1,)), ((), ())),
        preferred_element_type=F32,
    ).astype(BF16)


    for one in loads[1:]:
        one.wait()
    def wb_tiles(i, c):
        for k in range(8):
            rows_to_tiles(wb_in, wb, i * 8 + k, skus // 128)
        return c
    lax.fori_loop(0, skus // 1024, wb_tiles, 0)

    acc[...] = jnp.zeros_like(acc)
    each_group(nothing, lambda cols: category_add(bb[:, cols], cols), nothing)
    for m in range(blocks):
        spread_set(m, block_of(wc, m) * (block_of(bc, m) - category_total(m)))

    def set_p0(cols):
        p0[:, cols] = category_spread(cols)
    each_group(nothing, set_p0, lambda a: send_out(1, p0, a))

    wait_out(0)
    b0 = by_horizon(wr) * (by_horizon(br) - region_sum(0))
    breg[0] = b0
    region_spread(0, b0)
    send_back(0)
    wait_out(1)
    b1 = by_horizon(wr) * (region_sum(1) + counts * breg[0])
    breg[1] = b1
    region_spread(1, b1)
    send_back(1)

    acc[...] = jnp.zeros_like(acc)
    def set_v0(cols):
        x = p0[:, cols] + q[0, :, cols]
        v0[:, cols] = x
        add_moment(0, x * x)
        category_add(x, cols)
    each_group(lambda g: wait_back(0, g), set_v0, nothing)

    for m in range(blocks):
        spread_set(m, block_of(wc, m) * category_total(m))
    def set_u1(cols):
        u1[:, cols] = wb[:, cols] * v0[:, cols] + category_spread(cols)
    each_group(nothing, set_u1, lambda a: send_out(2, u1, a))

    acc[...] = jnp.zeros_like(acc)
    def set_v1(cols):
        y = u1[:, cols] + q[1, :, cols]
        v1[:, cols] = y
        add_moment(1, v0[:, cols] * y)
        add_moment(2, y * y)
        category_add(y, cols)
    each_group(lambda g: wait_back(1, g), set_v1, nothing)

    for m in range(blocks):
        spread_set(m, block_of(wc, m) * category_total(m))
    def set_u2(cols):
        u2[:, cols] = wb[:, cols] * v1[:, cols] + category_spread(cols)
    each_group(nothing, set_u2, lambda a: send_out(3, u2, a))

    wait_out(2)
    b2 = by_horizon(wr) * (region_sum(2) + counts * breg[1])
    breg[0] = b2
    region_spread(2, b2)
    send_back(2)
    wait_out(3)
    total3 = region_sum(3) + counts * breg[0]
    b3 = by_horizon(wr) * total3
    erow[...] = total3 * b3
    region_spread(3, b3)
    send_back(3)

    acc[...] = jnp.zeros_like(acc)
    def set_v2(cols):
        z = u2[:, cols] + q[2, :, cols]
        tt[:, cols] = z
        add_moment(3, v1[:, cols] * z)
        add_moment(4, z * z)
        add_moment(5, wb[:, cols] * z * z)
        category_add(z, cols)
    each_group(lambda g: wait_back(2, g), set_v2, nothing)

    energy = jnp.zeros((horizon, INNER), F32)
    for m in range(blocks):
        total = category_total(m)
        a3 = block_of(wc, m) * total
        energy = energy + total * a3
        spread_set(m, a3)

    lanes = lax.broadcasted_iota(jnp.int32, (1, 128), 1)
    row = jnp.zeros((1, 128), F32)
    for k in range(6):
        value = jnp.sum(mom[k, :, :], keepdims=True)
        if k == 5:
            value = value + (jnp.sum(energy, keepdims=True) + jnp.sum(erow[...], keepdims=True))
        row = jnp.where(lanes == k, value, row)
    arow[...] = row
    def reduce_send(a, c):
        send_group(a, lambda p: arow, ared.at[me], send_a, recv_a)
        return c
    lax.fori_loop(0, ns, reduce_send, 0)

    def set_rest(cols):
        p0[:, cols] = wb[:, cols] * tt[:, cols] + category_spread(cols)
    pltpu.make_async_copy(shape.at[pl.ds(0, n - 1)], shape.at[pl.ds(0, n - 1)], send_f.at[1]).wait()
    each_group(nothing, set_rest, nothing)

    pltpu.make_async_copy(ared, ared, recv_a).wait()
    high, low = ared[...], jnp.zeros((n, 1, 128), F32)
    while high.shape[0] > 1:
        half = high.shape[0] // 2
        high, low = pair_add((high[:half], low[:half]), (high[half:], low[half:]))
    high, low = high[0], low[0]
    moments = [(high[:, k:k + 1], low[:, k:k + 1]) for k in range(6)]
    (c1, c2, c3), (e0, e1, e2) = step_coefficients(moments)

    def finish(cols):
        x0, x1, x2 = v0[:, cols], v1[:, cols], tt[:, cols]
        x3 = p0[:, cols] + q[3, :, cols]
        return (x0 + c1 * x1 + c2 * x2 + c3 * x3, bb[:, cols] + (e0 * x0 + e1 * x1 + e2 * x2))

    def finish_group(a, c):
        g = st_of(a)
        wait_back(3, g)
        def inner(i, d):
            first_tile = (g * subs + i) * (WIDTH // 128)
            out_res, out_rec = finish(columns(g * subs + i, WIDTH))
            for k in range(WIDTH // 128):
                at = pl.ds(first_tile + k, horizon, stride=skus // 128)
                res[at, :] = out_res[:, 128 * k:128 * (k + 1)]
                rec[at, :] = out_rec[:, 128 * k:128 * (k + 1)]
            return d
        return lax.fori_loop(0, subs, inner, c)
    lax.fori_loop(0, ns, finish_group, 0)

    for f in (0, 2, 3):
        pltpu.make_async_copy(shape.at[pl.ds(0, n - 1)], shape.at[pl.ds(0, n - 1)], send_f.at[f]).wait()
    for f in range(4):
        pltpu.make_async_copy(shape.at[pl.ds(0, n - 1)], shape.at[pl.ds(0, n - 1)], send_q.at[f]).wait()
    pltpu.make_async_copy(ared.at[pl.ds(0, n - 1)], ared.at[pl.ds(0, n - 1)], send_a).wait()


def hand_on(rec, res, rec_out, res_out, rec_held, res_held, sems):
    height = rec.shape[0] // PARTS
    def piece(k, i, src, dst):
        at = pl.ds(i * height, height)
        return pltpu.make_async_copy(src.at[at], dst.at[at], sems.at[k, i])
    pairs = [(k, i) for i in range(PARTS) for k in range(2)]
    ends = ((rec, rec_held, rec_out), (res, res_held, res_out))
    for k, i in pairs:
        piece(k, i, ends[k][0], ends[k][1]).start()
    for k, i in pairs:
        piece(k, i, ends[k][0], ends[k][1]).wait()
        piece(k, i, ends[k][1], ends[k][2]).start()
    for k, i in pairs:
        piece(k, i, ends[k][1], ends[k][2]).wait()


def on_device(ns, nk, bb, wb, bc, wc, br, wr, cm, rm):
    n = ns * nk
    _, horizon, skus = bb.shape
    n_cat = bc.shape[2]
    regions, _, wide = br.shape
    blocks = n_cat // INNER
    vmem = pl.BlockSpec(memory_space=pltpu.VMEM)
    field = jax.ShapeDtypeStruct((horizon * skus // 128, 128), F32)
    rows = 3 * 16 * blocks
    rec, res = pl.pallas_call(
        functools.partial(kernel, ns, nk),
        out_shape=(field, field),
        in_specs=[pl.BlockSpec(memory_space=pltpu.HBM)] * 6 + [vmem] * 2,
        out_specs=(vmem, vmem),
        scratch_shapes=[
            *[pltpu.VMEM((horizon * skus // 128, 128), F32)] * 2,
            *[pltpu.VMEM((horizon * n_cat // 128, 128), F32)] * 2,
            *[pltpu.VMEM((horizon, regions, wide), F32)] * 2,
            pltpu.VMEM((INNER, skus), BF16),
            pltpu.VMEM((rows, WIDTH), BF16),
            pltpu.VMEM((rows, INNER), BF16),
            pltpu.VMEM((rows, INNER), F32),
            *[pltpu.VMEM((horizon, skus), F32)] * 8,
            pltpu.VMEM((4, horizon, skus), F32),
            pltpu.VMEM((4, n * 16, wide), F32),
            pltpu.VMEM((4, n * 16, wide), F32),
            pltpu.VMEM((n, horizon, wide), F32),
            pltpu.VMEM((2, regions, horizon * wide), F32),
            pltpu.VMEM((6, horizon, 128), F32),
            pltpu.VMEM((regions, horizon * wide), F32),
            pltpu.VMEM((1, 128), F32),
            pltpu.VMEM((n, 1, 128), F32),
            pltpu.SemaphoreType.DMA((4,)),
            pltpu.SemaphoreType.DMA((4,)),
            pltpu.SemaphoreType.DMA((4,)),
            pltpu.SemaphoreType.DMA((4, ns)),
            pltpu.SemaphoreType.DMA,
            pltpu.SemaphoreType.DMA,
            pltpu.SemaphoreType.DMA((6,)),
        ],
        compiler_params=pltpu.CompilerParams(
            collective_id=0, has_side_effects=True, vmem_limit_bytes=56 * 2**20
        ),
    )(
        bb.reshape(-1, 128), wb.reshape(-1, 128), bc.reshape(-1, 128), wc.reshape(-1, 128),
        br.transpose(1, 0, 2), wr.transpose(1, 0, 2), cm.reshape(1, skus), rm.reshape(1, n),
    )
    hbm = pl.BlockSpec(memory_space=pltpu.HBM)
    plain = jax.ShapeDtypeStruct(rec.shape, F32)
    rec, res = pl.pallas_call(
        hand_on, out_shape=(plain, plain), in_specs=[hbm] * 2, out_specs=(hbm, hbm),
        scratch_shapes=[*[pltpu.VMEM(rec.shape, F32)] * 2, pltpu.SemaphoreType.DMA((2, PARTS))],
    )(rec, res)
    return rec.reshape(1, horizon, skus), res.reshape(1, horizon, skus)


def solution(mesh):
    ns, nk = mesh.shape["store"], mesh.shape["sku"]
    split = P(("store", "sku"), None, None)
    by_sku = P(None, None, ("store", "sku"))
    return jax.shard_map(
        functools.partial(on_device, ns, nk), mesh=mesh,
        in_specs=(split, split, split, split, by_sku, by_sku, P(), P()),
        out_specs=(split, split), check_vma=False,
    )
```
